32 devices in a mesh: dp: 2 (over x), ctx: 16 (over z, y, core).
Axes of the slice: x: 2, y: 2, z: 4, core: 2. Of those that a mesh axis runs over, the one named last changes fastest.
Arguments:
- gate_outer: bfloat16 [2, 512, 2048], P('dp', None, 'ctx'), may hold values from -6 to 6
- gate_inner: bfloat16 [2, 512, 2048], P('dp', None, 'ctx'), may hold values from -6 to 6
- values_in: bfloat16 [2, 512, 2048], P('dp', None, 'ctx'), may hold values from -6 to 6
- cotangent: bfloat16 [2, 512, 2048], P('dp', None, 'ctx'), may hold values from -6 to 6
- filter_taps: bfloat16 [512, 2048], P(None, 'ctx'), may hold values from -2 to 2, as said below
- skip_gain: float32 [512], replicated, may hold values from 0.3 to 3
Outputs:
- hyena_result_array: bfloat16 [2, 512, 2048], P('dp', None, 'ctx')
- grad_outer: bfloat16 [2, 512, 2048], P('dp', None, 'ctx')
- grad_inner: bfloat16 [2, 512, 2048], P('dp', None, 'ctx')
- grad_values: bfloat16 [2, 512, 2048], P('dp', None, 'ctx')
- filter_grad: float32 [512, 2048], P(None, 'ctx')
The draws below stay inside these ranges and needn't reach their ends.
Inputs may be any that keep to these rules, and one draw needn't show every extreme that they name: `filter_taps`: one filter of 2048 taps for each channel.
All inputs are finite; a program needn't handle non-finite values.
Results may differ from the reference program's by a relative error of at most 0.011.
Values may be sent and summed in bfloat16 or wider, within the bound.
A program may use at most 64 MiB of HBM per device.

```python
import math
import jax
import jax.numpy as jnp
from jax import lax

C = 512
SEQ = 2048
SEQS = 2
N_DP = 2


def draw_filter_taps(key, part):
    key = jax.random.fold_in(key, 7)
    keys = jax.random.split(key, 6)
    slow_share = 0.5
    is_slow = jax.random.uniform(keys[0], (C, 1)) < slow_share
    slow_rate = jnp.exp(jax.random.uniform(keys[1], (C, 1), jnp.float32, jnp.log(0.05 / SEQ), jnp.log(2.3 / SEQ)))
    fast_rate = 2.3 / jax.random.uniform(keys[2], (C, 1), jnp.float32, 30.0, 50.0)
    rate = jnp.where(is_slow, slow_rate, fast_rate)
    nucleotide_offset = jnp.arange(SEQ, dtype=jnp.float32)[None, :]
    envelope = jnp.exp(-rate * nucleotide_offset) * jnp.sqrt(2.0 * rate + 1.0 / SEQ)
    accelerator_places = jax.random.uniform(keys[3], (C, 3), jnp.float32, 0.0, 1.0 * SEQ)
    discarded_lines = jax.random.uniform(keys[4], (C, 3), jnp.float32, 0.5, 0.8)
    multiplier_coefficient = jnp.ones((C, SEQ), jnp.float32)
    for contiguous_span_extent in range(3):
        multiplier_coefficient = multiplier_coefficient * jnp.where(nucleotide_offset >= accelerator_places[:, contiguous_span_extent:contiguous_span_extent + 1], discarded_lines[:, contiguous_span_extent:contiguous_span_extent + 1], 1.0)
    noise = jnp.clip(jax.random.normal(keys[5], (C, SEQ), jnp.float32), -4.0, 4.0)
    return (envelope * multiplier_coefficient * noise).astype(jnp.bfloat16)


def block_scale(rng, extent, cuts, low, largest):
    factor_of = 1.0
    for position, blocks in cuts:
        draws = jax.random.uniform(jax.random.fold_in(jax.random.fold_in(rng, 6), position), (blocks,), jnp.float32, low / len(cuts), largest / len(cuts))
        factor_of = factor_of * jnp.repeat(jnp.exp(draws), extent[position] // blocks).reshape((-1,) + (1,) * (len(extent) - 1 - position))
    return factor_of


def centred(own_key, extent, scale, most, cuts=(), kind=jnp.bfloat16):
    array = scale * jax.random.normal(own_key, extent, jnp.float32)
    if cuts:
        array = array * block_scale(own_key, extent, cuts, -0.22, 0.18)
    return jnp.clip(array, -most, most).astype(kind)


def setup_inputs(seed: int = 0) -> dict:
    streams_of = jax.random.split(jax.random.key(seed), 7)
    return {
        "gate_outer": centred(streams_of[0], (SEQS, C, SEQ), 1.0, 6.0, ((0, 2), (2, 16))),
        "gate_inner": centred(streams_of[1], (SEQS, C, SEQ), 1.0, 6.0, ((0, 2), (2, 16))),
        "values_in": centred(streams_of[2], (SEQS, C, SEQ), 1.0, 6.0, ((0, 2), (2, 16))),
        "cotangent": centred(streams_of[3], (SEQS, C, SEQ), 1.0, 6.0, ((0, 2), (2, 16))),
        "filter_taps": draw_filter_taps(jax.random.fold_in(streams_of[6], 71), 0),
        "skip_gain": jnp.clip(jnp.exp(jax.random.uniform(streams_of[5], (C,), jnp.float32, math.log(0.3), math.log(3.0))), 0.3, 3.0),
    }


def reference(gate_outer, gate_inner, values_in, cotangent, filter_taps, skip_gain):
    length = 2 * SEQ
    spec_h = jnp.fft.fft(filter_taps.astype(jnp.float32), n=length, axis=1)
    gain = skip_gain[:, None]

    def step(total, item):
        outer, inner, values, cotan = item
        mixed = (inner.astype(jnp.float32) * values.astype(jnp.float32)).astype(jnp.bfloat16)
        back_in = (cotan.astype(jnp.float32) * outer.astype(jnp.float32)).astype(jnp.bfloat16)
        mixed_f = mixed.astype(jnp.float32)
        back_f = back_in.astype(jnp.float32)
        spec_u = jnp.fft.fft(mixed_f, n=length, axis=1)
        spec_d = jnp.fft.fft(back_f, n=length, axis=1)
        conv_part = jnp.fft.ifft(spec_u * spec_h, axis=1).real[:, :SEQ].astype(jnp.float32).astype(jnp.bfloat16)
        back_part = jnp.fft.ifft(jnp.conj(spec_h) * spec_d, axis=1).real[:, :SEQ].astype(jnp.float32).astype(jnp.bfloat16)
        term = jnp.fft.ifft(spec_d * jnp.conj(spec_u), axis=1).real[:, :SEQ].astype(jnp.float32)
        state = conv_part.astype(jnp.float32) + gain * mixed_f
        layer = (outer.astype(jnp.float32) * state).astype(jnp.bfloat16)
        g_outer = (cotan.astype(jnp.float32) * state).astype(jnp.bfloat16)
        g_mixed = back_part.astype(jnp.float32) + gain * back_f
        g_inner = (g_mixed * values.astype(jnp.float32)).astype(jnp.bfloat16)
        g_values = (g_mixed * inner.astype(jnp.float32)).astype(jnp.bfloat16)
        return (total + term, (layer, g_outer, g_inner, g_values))
    start = jnp.zeros((C, SEQ), jnp.float32)
    total, outs = lax.scan(step, start, (gate_outer, gate_inner, values_in, cotangent))
    filter_grad = total * (1.0 / math.sqrt(N_DP * SEQ))
    return (outs[0], outs[1], outs[2], outs[3], filter_grad)
```

```python
import functools
import math

import jax
import jax.numpy as jnp
import numpy as np
from jax import lax
from jax.experimental import pallas as pl
from jax.experimental.pallas import tpu as pltpu
from jax.sharding import PartitionSpec as P

highest = lax.Precision.HIGHEST
inner_order = 128
MESH = pl.DeviceIdType.MESH
F32 = jnp.float32
BF16 = jnp.bfloat16


def tables(order, count):
    rows = lax.broadcasted_iota(jnp.int32, (order, count), 0)
    cols = lax.broadcasted_iota(jnp.int32, (order, count), 1)
    angle = (rows * cols % order).astype(jnp.float32) * (2.0 * math.pi / order)
    return (jnp.cos(angle), jnp.sin(angle))


def twiddles(outer_order, total):
    rows = lax.broadcasted_iota(jnp.int32, (outer_order, inner_order), 0)
    cols = lax.broadcasted_iota(jnp.int32, (outer_order, inner_order), 1)
    angle = (rows * cols % total).astype(jnp.float32) * (2.0 * math.pi / total)
    return (jnp.cos(angle), jnp.sin(angle))


def forward_spectrum(signal):
    chans, seq = signal.shape
    outer_order = 2 * seq // inner_order
    half = outer_order // 2
    block_groups = signal.reshape(chans, half, inner_order)
    cos_p, sin_p = tables(outer_order, half)
    a_re = jnp.einsum("kn,cnm->ckm", cos_p, block_groups, precision=highest)
    a_im = -jnp.einsum("kn,cnm->ckm", sin_p, block_groups, precision=highest)
    tw_c, tw_s = twiddles(outer_order, outer_order * inner_order)
    b_re = a_re * tw_c + a_im * tw_s
    b_im = a_im * tw_c - a_re * tw_s
    cos_q, sin_q = tables(inner_order, inner_order)
    x_re = jnp.einsum("ckn,nm->ckm", b_re, cos_q, precision=highest) + jnp.einsum(
        "ckn,nm->ckm", b_im, sin_q, precision=highest
    )
    x_im = jnp.einsum("ckn,nm->ckm", b_im, cos_q, precision=highest) - jnp.einsum(
        "ckn,nm->ckm", b_re, sin_q, precision=highest
    )
    return (x_re, x_im)


def inverse_real_part(y_re, y_im):
    chans, outer_order, _ = y_re.shape
    half = outer_order // 2
    total = outer_order * inner_order
    cos_q, sin_q = tables(inner_order, inner_order)
    z_re = jnp.einsum("ckn,nm->ckm", y_re, cos_q, precision=highest) - jnp.einsum(
        "ckn,nm->ckm", y_im, sin_q, precision=highest
    )
    z_im = jnp.einsum("ckn,nm->ckm", y_im, cos_q, precision=highest) + jnp.einsum(
        "ckn,nm->ckm", y_re, sin_q, precision=highest
    )
    tw_c, tw_s = twiddles(outer_order, total)
    w_re = z_re * tw_c - z_im * tw_s
    w_im = z_im * tw_c + z_re * tw_s
    cos_p, sin_p = tables(outer_order, half)
    result = jnp.einsum("kn,ckm->cnm", cos_p, w_re, precision=highest) - jnp.einsum(
        "kn,ckm->cnm", sin_p, w_im, precision=highest
    )
    return (result * (1.0 / total)).reshape(chans, half * inner_order)


def general_exchange(mixed, back_in, filter_taps):
    ctx_count = lax.axis_size("ctx")
    dp_count = lax.axis_size("dp")
    seq = mixed.shape[1] * ctx_count
    norm_scale = 1.0 / math.sqrt(dp_count * seq)
    mixed_ch, back_ch, taps_ch = (
        lax.all_to_all(mixed, "ctx", split_axis=0, concat_axis=1, tiled=True),
        lax.all_to_all(back_in, "ctx", split_axis=0, concat_axis=1, tiled=True),
        lax.all_to_all(filter_taps, "ctx", split_axis=0, concat_axis=1, tiled=True),
    )
    h_re, h_im = forward_spectrum(taps_ch.astype(jnp.float32))
    u_re, u_im = forward_spectrum(mixed_ch.astype(jnp.float32))
    d_re, d_im = forward_spectrum(back_ch.astype(jnp.float32))
    conv_ch = inverse_real_part(u_re * h_re - u_im * h_im, u_re * h_im + u_im * h_re).astype(
        jnp.bfloat16
    )
    back_ch_out = inverse_real_part(h_re * d_re + h_im * d_im, h_re * d_im - h_im * d_re).astype(
        jnp.bfloat16
    )
    conv_seq, back_seq = (
        lax.all_to_all(conv_ch, "ctx", split_axis=1, concat_axis=0, tiled=True),
        lax.all_to_all(back_ch_out, "ctx", split_axis=1, concat_axis=0, tiled=True),
    )
    g_re = d_re * u_re + d_im * u_im
    g_im = d_im * u_re - d_re * u_im
    term = inverse_real_part(g_re, g_im)
    summed = lax.psum(term, "dp")
    filter_grad = lax.all_to_all(
        summed * norm_scale, "ctx", split_axis=1, concat_axis=0, tiled=True
    )
    return conv_seq, back_seq, filter_grad


def two_parts(table):
    high = table.astype(np.float32).astype(BF16)
    low = (table - high.astype(np.float64)).astype(np.float32).astype(BF16)
    return np.stack([np.asarray(high), np.asarray(low)])


@functools.lru_cache(maxsize=None)
def kernel_tables(blocks, group, width):
    total = 2 * blocks * width
    n = np.arange(blocks)
    angle = 2.0 * np.pi * ((np.outer(2 * n + 1, n)) % (4 * blocks)) / (4 * blocks)
    unit = np.eye(group)
    outer_f = np.concatenate([np.kron(np.cos(angle), unit), np.kron(-np.sin(angle), unit)], axis=0)
    outer_i = outer_f.T * (2.0 / total)
    m = np.arange(width)
    angle_in = 2.0 * np.pi * (np.outer(m, m) % width) / width
    c, s = np.cos(angle_in), np.sin(angle_in)
    inner_f = np.block([[c, -s], [s, c]])
    inner_i = np.block([[c, s], [-s, c]])
    angle_tw = 2.0 * np.pi * np.outer(2 * n + 1, m) / (2.0 * total)
    tw = np.stack([np.cos(angle_tw), np.sin(angle_tw)])
    tw = np.repeat(tw, group, axis=1).astype(np.float32)
    return two_parts(outer_f), two_parts(outer_i), two_parts(inner_f), two_parts(inner_i), tw


def dot(a, b):
    return jnp.dot(a, b, preferred_element_type=F32)


def split(x):
    high = x.astype(BF16)
    return high, (x - high.astype(F32)).astype(BF16)


def kernel(
    dp_count,
    ctx_count,
    outer_ref,
    inner_ref,
    values_ref,
    cotan_ref,
    taps_ref,
    outer_f_hbm,
    outer_i_hbm,
    inner_f_hbm,
    inner_i_hbm,
    tw_hbm,
    conv_out,
    back_out,
    grad_out,
    mixed,
    back_in,
    recv_u,
    recv_d,
    recv_h,
    sent_conv,
    sent_back,
    sent_grad,
    outer_f,
    outer_i,
    inner_f,
    inner_i,
    tw,
    table_sems,
    send_sems,
    recv_sems,
):
    ranks = dp_count * ctx_count
    chans, width = mixed.shape
    group = chans // ranks
    rows = ctx_count * group
    my_dp = lax.axis_index("dp")
    my_ctx = lax.axis_index("ctx")
    me = my_dp * ctx_count + my_ctx

    barrier = pltpu.get_barrier_semaphore()

    def greet(i, carry):
        peer = lax.rem(me + i, ranks)
        pl.semaphore_signal(
            barrier,
            inc=1,
            device_id=(peer // ctx_count, lax.rem(peer, ctx_count)),
            device_id_type=MESH,
        )
        return carry

    lax.fori_loop(1, ranks, greet, 0)

    table_copies = [
        pltpu.make_async_copy(src, dst, table_sems.at[i])
        for i, (src, dst) in enumerate(
            [
                (outer_f_hbm, outer_f),
                (inner_f_hbm, inner_f),
                (tw_hbm, tw),
                (inner_i_hbm, inner_i),
                (outer_i_hbm, outer_i),
            ]
        )
    ]
    for copy in table_copies:
        copy.start()

    mixed[...] = (inner_ref[...].astype(F32) * values_ref[...].astype(F32)).astype(BF16)
    back_in[...] = (cotan_ref[...].astype(F32) * outer_ref[...].astype(F32)).astype(BF16)
    pl.semaphore_wait(barrier, ranks - 1)

    def chunk(ref, index):
        return ref.at[pl.ds(pl.multiple_of(index * group, group), group)]

    def to_peer(src, dst, which, peer):
        return pltpu.make_async_remote_copy(
            src_ref=src,
            dst_ref=dst,
            send_sem=send_sems.at[which],
            recv_sem=recv_sems.at[which],
            device_id=(peer // ctx_count, lax.rem(peer, ctx_count)),
            device_id_type=MESH,
        )

    def send_taps(i, carry):
        ctx = lax.rem(my_ctx + i, ctx_count)
        peer = my_dp * ctx_count + ctx
        to_peer(chunk(taps_ref, peer), chunk(recv_h, my_ctx), 0, peer).start()
        return carry

    def send_mixed(i, carry):
        peer = lax.rem(me + i, ranks)
        to_peer(chunk(mixed, peer), chunk(recv_u, me), 1, peer).start()
        return carry

    def send_back(i, carry):
        peer = lax.rem(me + i, ranks)
        to_peer(chunk(back_in, peer), chunk(recv_d, me), 2, peer).start()
        return carry

    lax.fori_loop(1, ctx_count, send_taps, 0)
    lax.fori_loop(1, ranks, send_mixed, 0)
    lax.fori_loop(1, ranks, send_back, 0)
    pltpu.make_async_copy(chunk(taps_ref, me), chunk(recv_h, my_ctx), recv_sems.at[0]).start()
    pltpu.make_async_copy(chunk(mixed, me), chunk(recv_u, me), recv_sems.at[1]).start()
    pltpu.make_async_copy(chunk(back_in, me), chunk(recv_d, me), recv_sems.at[2]).start()

    def arrived(ref, which):
        pltpu.make_async_copy(ref, ref, recv_sems.at[which]).wait()

    def spectra(signals):
        count = len(signals)
        side = jnp.concatenate(signals, axis=1)
        a = dot(outer_f[0], side) + dot(outer_f[1], side)
        parts = []
        for s in range(count):
            re = a[:rows, s * width : (s + 1) * width]
            im = a[rows:, s * width : (s + 1) * width]
            parts.append(
                jnp.concatenate([re * tw[0] + im * tw[1], im * tw[0] - re * tw[1]], axis=1)
            )
        high, low = split(jnp.concatenate(parts, axis=0))
        x = dot(high, inner_f[0]) + (dot(high, inner_f[1]) + dot(low, inner_f[0]))
        return [
            (x[s * rows : (s + 1) * rows, :width], x[s * rows : (s + 1) * rows, width:])
            for s in range(count)
        ]

    def signals_of(products):
        count = len(products)
        high, low = split(
            jnp.concatenate([jnp.concatenate([re, im], axis=1) for re, im in products], axis=0)
        )
        z = dot(high, inner_i[0]) + (dot(high, inner_i[1]) + dot(low, inner_i[0]))
        parts = []
        for s in range(count):
            re = z[s * rows : (s + 1) * rows, :width]
            im = z[s * rows : (s + 1) * rows, width:]
            parts.append(
                jnp.concatenate([re * tw[0] - im * tw[1], im * tw[0] + re * tw[1]], axis=0)
            )
        high, low = split(jnp.concatenate(parts, axis=1))
        y = dot(outer_i[0], high) + (dot(outer_i[1], high) + dot(outer_i[0], low))
        return [y[:, s * width : (s + 1) * width] for s in range(count)]

    def times(a, b):
        return a[0] * b[0] - a[1] * b[1], a[0] * b[1] + a[1] * b[0]

    def times_conj(a, b):
        return a[0] * b[0] + a[1] * b[1], a[1] * b[0] - a[0] * b[1]

    def return_sequences(src, dst, which):
        def step(i, carry):
            peer = lax.rem(me + i, ranks)
            to_peer(chunk(src, peer), chunk(dst, me), which, peer).start()
            return carry

        lax.fori_loop(1, ranks, step, 0)
        pltpu.make_async_copy(chunk(src, me), chunk(dst, me), recv_sems.at[which]).start()

    arrived(recv_h, 0)
    arrived(recv_u, 1)
    for copy in table_copies:
        copy.wait()
    spec = spectra(
        [recv_h[...]] + [recv_u[s * rows : (s + 1) * rows] for s in range(dp_count)]
    )
    spec_h, spec_u = spec[0], spec[1:]
    for s, y in enumerate(signals_of([times(u, spec_h) for u in spec_u])):
        sent_conv[s * rows : (s + 1) * rows] = y.astype(BF16)
    return_sequences(sent_conv, conv_out, 3)

    arrived(recv_d, 2)
    spec_d = spectra([recv_d[s * rows : (s + 1) * rows] for s in range(dp_count)])
    for s, y in enumerate(signals_of([times_conj(d, spec_h) for d in spec_d])):
        sent_back[s * rows : (s + 1) * rows] = y.astype(BF16)
    return_sequences(sent_back, back_out, 4)

    terms = [times_conj(d, u) for d, u in zip(spec_d, spec_u)]
    term = (sum(t[0] for t in terms), sum(t[1] for t in terms))
    norm_scale = 1.0 / math.sqrt(dp_count * ctx_count * width)
    sent_grad[...] = (signals_of([term])[0] * norm_scale).astype(BF16)

    def send_grad(i, carry):
        peer = lax.rem(me + i, ranks)
        to_peer(chunk(sent_grad, lax.rem(peer, ctx_count)), chunk(grad_out, me), 5, peer).start()
        return carry

    lax.fori_loop(1, ranks, send_grad, 0)
    pltpu.make_async_copy(chunk(sent_grad, my_ctx), chunk(grad_out, me), recv_sems.at[5]).start()

    arrived(conv_out, 3)
    arrived(back_out, 4)
    arrived(grad_out, 5)
    for which, count in ((0, ctx_count), (1, ranks), (2, ranks), (3, ranks), (4, ranks), (5, ranks)):
        part = mixed.at[pl.ds(0, (count - 1) * group)]
        pltpu.make_async_copy(part, part, send_sems.at[which]).wait()


def kernel_exchange(outer, inner, values, cotan, filter_taps):
    ctx_count = lax.axis_size("ctx")
    dp_count = lax.axis_size("dp")
    chans, width = outer.shape
    group = chans // (dp_count * ctx_count)
    rows = ctx_count * group
    constants = kernel_tables(ctx_count, group, width)
    vmem = pl.BlockSpec(memory_space=pltpu.VMEM)
    anywhere = pl.BlockSpec(memory_space=pl.ANY)
    local = jax.ShapeDtypeStruct((chans, width), BF16)
    signal = pltpu.VMEM((chans, width), BF16)
    one = pltpu.VMEM((rows, width), BF16)
    return pl.pallas_call(
        functools.partial(kernel, dp_count, ctx_count),
        out_shape=(local, local, local),
        in_specs=[vmem] * 5 + [anywhere] * 5,
        out_specs=(vmem, vmem, vmem),
        scratch_shapes=[signal, signal, signal, signal, one, signal, signal, one]
        + [pltpu.VMEM(t.shape, t.dtype) for t in constants]
        + [
            pltpu.SemaphoreType.DMA((5,)),
            pltpu.SemaphoreType.DMA((6,)),
            pltpu.SemaphoreType.DMA((6,)),
        ],
        compiler_params=pltpu.CompilerParams(
            collective_id=0, has_side_effects=True, vmem_limit_bytes=48 * 1024 * 1024
        ),
        cost_estimate=pl.CostEstimate(
            flops=2_000_000_000, bytes_accessed=4_000_000, transcendentals=0
        ),
    )(outer, inner, values, cotan, filter_taps, *[jnp.asarray(t) for t in constants])


def on_device(gate_outer, gate_inner, values_in, cotangent, filter_taps, skip_gain):
    outer = gate_outer[0]
    inner = gate_inner[0]
    values = values_in[0]
    cotan = cotangent[0]
    ranks = lax.axis_size("ctx") * lax.axis_size("dp")
    mixed = (inner.astype(F32) * values.astype(F32)).astype(BF16)
    back_in = (cotan.astype(F32) * outer.astype(F32)).astype(BF16)
    if outer.shape[0] % (16 * ranks) == 0 and outer.shape[1] == inner_order:
        conv_seq, back_seq, filter_grad = kernel_exchange(outer, inner, values, cotan, filter_taps)
    else:
        conv_seq, back_seq, filter_grad = general_exchange(mixed, back_in, filter_taps)
    gain = skip_gain[:, None]
    state = conv_seq.astype(F32) + gain * mixed.astype(F32)
    layer = (outer.astype(F32) * state).astype(BF16)
    g_outer = (cotan.astype(F32) * state).astype(BF16)
    g_mixed = back_seq.astype(F32) + gain * back_in.astype(F32)
    g_inner = (g_mixed * values.astype(F32)).astype(BF16)
    g_values = (g_mixed * inner.astype(F32)).astype(BF16)
    return (layer[None], g_outer[None], g_inner[None], g_values[None], filter_grad.astype(F32))


def solution(mesh):
    placed = (
        P("dp", None, "ctx"),
        P("dp", None, "ctx"),
        P("dp", None, "ctx"),
        P("dp", None, "ctx"),
        P(None, "ctx"),
        P(),
    )
    return jax.shard_map(
        on_device,
        mesh=mesh,
        in_specs=placed,
        out_specs=(
            P("dp", None, "ctx"),
            P("dp", None, "ctx"),
            P("dp", None, "ctx"),
            P("dp", None, "ctx"),
            P(None, "ctx"),
        ),
        check_vma=False,
    )
```

```python
import functools
import math

import jax
import jax.numpy as jnp
import numpy as np
from jax import lax
from jax.experimental import pallas as pl
from jax.experimental.pallas import tpu as pltpu
from jax.sharding import PartitionSpec as P

highest = lax.Precision.HIGHEST
inner_order = 128
MESH = pl.DeviceIdType.MESH
F32 = jnp.float32
BF16 = jnp.bfloat16


def tables(order, count):
    rows = lax.broadcasted_iota(jnp.int32, (order, count), 0)
    cols = lax.broadcasted_iota(jnp.int32, (order, count), 1)
    angle = (rows * cols % order).astype(jnp.float32) * (2.0 * math.pi / order)
    return (jnp.cos(angle), jnp.sin(angle))


def twiddles(outer_order, total):
    rows = lax.broadcasted_iota(jnp.int32, (outer_order, inner_order), 0)
    cols = lax.broadcasted_iota(jnp.int32, (outer_order, inner_order), 1)
    angle = (rows * cols % total).astype(jnp.float32) * (2.0 * math.pi / total)
    return (jnp.cos(angle), jnp.sin(angle))


def forward_spectrum(signal):
    chans, seq = signal.shape
    outer_order = 2 * seq // inner_order
    half = outer_order // 2
    block_groups = signal.reshape(chans, half, inner_order)
    cos_p, sin_p = tables(outer_order, half)
    a_re = jnp.einsum("kn,cnm->ckm", cos_p, block_groups, precision=highest)
    a_im = -jnp.einsum("kn,cnm->ckm", sin_p, block_groups, precision=highest)
    tw_c, tw_s = twiddles(outer_order, outer_order * inner_order)
    b_re = a_re * tw_c + a_im * tw_s
    b_im = a_im * tw_c - a_re * tw_s
    cos_q, sin_q = tables(inner_order, inner_order)
    x_re = jnp.einsum("ckn,nm->ckm", b_re, cos_q, precision=highest) + jnp.einsum(
        "ckn,nm->ckm", b_im, sin_q, precision=highest
    )
    x_im = jnp.einsum("ckn,nm->ckm", b_im, cos_q, precision=highest) - jnp.einsum(
        "ckn,nm->ckm", b_re, sin_q, precision=highest
    )
    return (x_re, x_im)


def inverse_real_part(y_re, y_im):
    chans, outer_order, _ = y_re.shape
    half = outer_order // 2
    total = outer_order * inner_order
    cos_q, sin_q = tables(inner_order, inner_order)
    z_re = jnp.einsum("ckn,nm->ckm", y_re, cos_q, precision=highest) - jnp.einsum(
        "ckn,nm->ckm", y_im, sin_q, precision=highest
    )
    z_im = jnp.einsum("ckn,nm->ckm", y_im, cos_q, precision=highest) + jnp.einsum(
        "ckn,nm->ckm", y_re, sin_q, precision=highest
    )
    tw_c, tw_s = twiddles(outer_order, total)
    w_re = z_re * tw_c - z_im * tw_s
    w_im = z_im * tw_c + z_re * tw_s
    cos_p, sin_p = tables(outer_order, half)
    result = jnp.einsum("kn,ckm->cnm", cos_p, w_re, precision=highest) - jnp.einsum(
        "kn,ckm->cnm", sin_p, w_im, precision=highest
    )
    return (result * (1.0 / total)).reshape(chans, half * inner_order)


def general_exchange(mixed, back_in, filter_taps):
    ctx_count = lax.axis_size("ctx")
    dp_count = lax.axis_size("dp")
    seq = mixed.shape[1] * ctx_count
    norm_scale = 1.0 / math.sqrt(dp_count * seq)
    mixed_ch, back_ch, taps_ch = (
        lax.all_to_all(mixed, "ctx", split_axis=0, concat_axis=1, tiled=True),
        lax.all_to_all(back_in, "ctx", split_axis=0, concat_axis=1, tiled=True),
        lax.all_to_all(filter_taps, "ctx", split_axis=0, concat_axis=1, tiled=True),
    )
    h_re, h_im = forward_spectrum(taps_ch.astype(jnp.float32))
    u_re, u_im = forward_spectrum(mixed_ch.astype(jnp.float32))
    d_re, d_im = forward_spectrum(back_ch.astype(jnp.float32))
    conv_ch = inverse_real_part(u_re * h_re - u_im * h_im, u_re * h_im + u_im * h_re).astype(
        jnp.bfloat16
    )
    back_ch_out = inverse_real_part(h_re * d_re + h_im * d_im, h_re * d_im - h_im * d_re).astype(
        jnp.bfloat16
    )
    conv_seq, back_seq = (
        lax.all_to_all(conv_ch, "ctx", split_axis=1, concat_axis=0, tiled=True),
        lax.all_to_all(back_ch_out, "ctx", split_axis=1, concat_axis=0, tiled=True),
    )
    g_re = d_re * u_re + d_im * u_im
    g_im = d_im * u_re - d_re * u_im
    term = inverse_real_part(g_re, g_im)
    summed = lax.psum(term, "dp")
    filter_grad = lax.all_to_all(
        summed * norm_scale, "ctx", split_axis=1, concat_axis=0, tiled=True
    )
    return conv_seq, back_seq, filter_grad


def two_parts(table):
    high = table.astype(np.float32).astype(BF16)
    low = (table - high.astype(np.float64)).astype(np.float32).astype(BF16)
    return np.stack([np.asarray(high), np.asarray(low)])


@functools.lru_cache(maxsize=None)
def kernel_tables(blocks, group, width):
    total = 2 * blocks * width
    n = np.arange(blocks)
    angle = 2.0 * np.pi * ((np.outer(2 * n + 1, n)) % (4 * blocks)) / (4 * blocks)
    unit = np.eye(group)
    outer_f = np.concatenate([np.kron(np.cos(angle), unit), np.kron(-np.sin(angle), unit)], axis=0)
    outer_i = outer_f.T * (2.0 / total)
    m = np.arange(width)
    angle_in = 2.0 * np.pi * (np.outer(m, m) % width) / width
    c, s = np.cos(angle_in), np.sin(angle_in)
    inner_f = np.block([[c, -s], [s, c]])
    inner_i = np.block([[c, s], [-s, c]])
    angle_tw = 2.0 * np.pi * np.outer(2 * n + 1, m) / (2.0 * total)
    tw = np.stack([np.cos(angle_tw), np.sin(angle_tw)])
    tw = np.repeat(tw, group, axis=1).astype(np.float32)
    return two_parts(outer_f), two_parts(outer_i), two_parts(inner_f), two_parts(inner_i), tw


def dot(a, b):
    return jnp.dot(a, b, preferred_element_type=F32)


def split(x):
    high = x.astype(BF16)
    return high, (x - high.astype(F32)).astype(BF16)


def kernel(
    dp_count,
    ctx_count,
    outer_hbm,
    inner_hbm,
    values_hbm,
    cotan_hbm,
    taps_hbm,
    outer_f_hbm,
    outer_i_hbm,
    inner_f_hbm,
    inner_i_hbm,
    tw_hbm,
    conv_out,
    back_out,
    grad_out,
    outer_ref,
    inner_ref,
    values_ref,
    cotan_ref,
    taps_ref,
    mixed,
    back_in,
    recv_u,
    recv_d,
    recv_h,
    sent_conv,
    sent_back,
    sent_grad,
    outer_f,
    outer_i,
    inner_f,
    inner_i,
    tw,
    input_sems,
    table_sems,
    send_sems,
    recv_sems,
):
    ranks = dp_count * ctx_count
    chans, width = mixed.shape
    group = chans // ranks
    rows = ctx_count * group
    my_dp = lax.axis_index("dp")
    my_ctx = lax.axis_index("ctx")
    me = my_dp * ctx_count + my_ctx

    input_copies = [
        pltpu.make_async_copy(src, dst, input_sems.at[i])
        for i, (src, dst) in enumerate(
            [
                (inner_hbm, inner_ref),
                (values_hbm, values_ref),
                (taps_hbm, taps_ref),
                (cotan_hbm, cotan_ref),
                (outer_hbm, outer_ref),
            ]
        )
    ]
    for copy in input_copies:
        copy.start()
    barrier = pltpu.get_barrier_semaphore()

    def greet(i, carry):
        peer = lax.rem(me + i, ranks)
        pl.semaphore_signal(
            barrier,
            inc=1,
            device_id=(peer // ctx_count, lax.rem(peer, ctx_count)),
            device_id_type=MESH,
        )
        return carry

    lax.fori_loop(1, ranks, greet, 0)

    table_copies = [
        pltpu.make_async_copy(src, dst, table_sems.at[i])
        for i, (src, dst) in enumerate(
            [
                (outer_f_hbm, outer_f),
                (inner_f_hbm, inner_f),
                (tw_hbm, tw),
                (inner_i_hbm, inner_i),
                (outer_i_hbm, outer_i),
            ]
        )
    ]
    for copy in table_copies:
        copy.start()

    for copy in input_copies:
        copy.wait()
    mixed[...] = (inner_ref[...].astype(F32) * values_ref[...].astype(F32)).astype(BF16)
    back_in[...] = (cotan_ref[...].astype(F32) * outer_ref[...].astype(F32)).astype(BF16)
    pl.semaphore_wait(barrier, ranks - 1)

    def chunk(ref, index):
        return ref.at[pl.ds(pl.multiple_of(index * group, group), group)]

    def to_peer(src, dst, which, peer):
        return pltpu.make_async_remote_copy(
            src_ref=src,
            dst_ref=dst,
            send_sem=send_sems.at[which],
            recv_sem=recv_sems.at[which],
            device_id=(peer // ctx_count, lax.rem(peer, ctx_count)),
            device_id_type=MESH,
        )

    def send_taps(i, carry):
        ctx = lax.rem(my_ctx + i, ctx_count)
        peer = my_dp * ctx_count + ctx
        to_peer(chunk(taps_ref, peer), chunk(recv_h, my_ctx), 0, peer).start()
        return carry

    def send_mixed(i, carry):
        peer = lax.rem(me + i, ranks)
        to_peer(chunk(mixed, peer), chunk(recv_u, me), 1, peer).start()
        return carry

    def send_back(i, carry):
        peer = lax.rem(me + i, ranks)
        to_peer(chunk(back_in, peer), chunk(recv_d, me), 2, peer).start()
        return carry

    lax.fori_loop(1, ctx_count, send_taps, 0)
    lax.fori_loop(1, ranks, send_mixed, 0)
    lax.fori_loop(1, ranks, send_back, 0)
    pltpu.make_async_copy(chunk(taps_ref, me), chunk(recv_h, my_ctx), recv_sems.at[0]).start()
    pltpu.make_async_copy(chunk(mixed, me), chunk(recv_u, me), recv_sems.at[1]).start()
    pltpu.make_async_copy(chunk(back_in, me), chunk(recv_d, me), recv_sems.at[2]).start()

    def arrived(ref, which):
        pltpu.make_async_copy(ref, ref, recv_sems.at[which]).wait()

    def spectra(signals):
        count = len(signals)
        side = jnp.concatenate(signals, axis=1)
        a = dot(outer_f[0], side) + dot(outer_f[1], side)
        parts = []
        for s in range(count):
            re = a[:rows, s * width : (s + 1) * width]
            im = a[rows:, s * width : (s + 1) * width]
            parts.append(
                jnp.concatenate([re * tw[0] + im * tw[1], im * tw[0] - re * tw[1]], axis=1)
            )
        high, low = split(jnp.concatenate(parts, axis=0))
        x = dot(high, inner_f[0]) + (dot(high, inner_f[1]) + dot(low, inner_f[0]))
        return [
            (x[s * rows : (s + 1) * rows, :width], x[s * rows : (s + 1) * rows, width:])
            for s in range(count)
        ]

    def signals_of(products):
        count = len(products)
        high, low = split(
            jnp.concatenate([jnp.concatenate([re, im], axis=1) for re, im in products], axis=0)
        )
        z = dot(high, inner_i[0]) + (dot(high, inner_i[1]) + dot(low, inner_i[0]))
        parts = []
        for s in range(count):
            re = z[s * rows : (s + 1) * rows, :width]
            im = z[s * rows : (s + 1) * rows, width:]
            parts.append(
                jnp.concatenate([re * tw[0] - im * tw[1], im * tw[0] + re * tw[1]], axis=0)
            )
        high, low = split(jnp.concatenate(parts, axis=1))
        y = dot(outer_i[0], high) + (dot(outer_i[1], high) + dot(outer_i[0], low))
        return [y[:, s * width : (s + 1) * width] for s in range(count)]

    def times(a, b):
        return a[0] * b[0] - a[1] * b[1], a[0] * b[1] + a[1] * b[0]

    def times_conj(a, b):
        return a[0] * b[0] + a[1] * b[1], a[1] * b[0] - a[0] * b[1]

    def return_sequences(src, dst, which):
        def step(i, carry):
            peer = lax.rem(me + i, ranks)
            to_peer(chunk(src, peer), chunk(dst, me), which, peer).start()
            return carry

        lax.fori_loop(1, ranks, step, 0)
        pltpu.make_async_copy(chunk(src, me), chunk(dst, me), recv_sems.at[which]).start()

    arrived(recv_h, 0)
    arrived(recv_u, 1)
    for copy in table_copies:
        copy.wait()
    spec = spectra(
        [recv_h[...]] + [recv_u[s * rows : (s + 1) * rows] for s in range(dp_count)]
    )
    spec_h, spec_u = spec[0], spec[1:]
    for s, y in enumerate(signals_of([times(u, spec_h) for u in spec_u])):
        sent_conv[s * rows : (s + 1) * rows] = y.astype(BF16)
    return_sequences(sent_conv, conv_out, 3)

    arrived(recv_d, 2)
    spec_d = spectra([recv_d[s * rows : (s + 1) * rows] for s in range(dp_count)])
    for s, y in enumerate(signals_of([times_conj(d, spec_h) for d in spec_d])):
        sent_back[s * rows : (s + 1) * rows] = y.astype(BF16)
    return_sequences(sent_back, back_out, 4)

    terms = [times_conj(d, u) for d, u in zip(spec_d, spec_u)]
    term = (sum(t[0] for t in terms), sum(t[1] for t in terms))
    norm_scale = 1.0 / math.sqrt(dp_count * ctx_count * width)
    sent_grad[...] = (signals_of([term])[0] * norm_scale).astype(BF16)

    def send_grad(i, carry):
        peer = lax.rem(me + i, ranks)
        to_peer(chunk(sent_grad, lax.rem(peer, ctx_count)), chunk(grad_out, me), 5, peer).start()
        return carry

    lax.fori_loop(1, ranks, send_grad, 0)
    pltpu.make_async_copy(chunk(sent_grad, my_ctx), chunk(grad_out, me), recv_sems.at[5]).start()

    arrived(conv_out, 3)
    arrived(back_out, 4)
    arrived(grad_out, 5)
    for which, count in ((0, ctx_count), (1, ranks), (2, ranks), (3, ranks), (4, ranks), (5, ranks)):
        part = mixed.at[pl.ds(0, (count - 1) * group)]
        pltpu.make_async_copy(part, part, send_sems.at[which]).wait()


def kernel_exchange(outer, inner, values, cotan, filter_taps):
    ctx_count = lax.axis_size("ctx")
    dp_count = lax.axis_size("dp")
    chans, width = outer.shape
    group = chans // (dp_count * ctx_count)
    rows = ctx_count * group
    constants = kernel_tables(ctx_count, group, width)
    vmem = pl.BlockSpec(memory_space=pltpu.VMEM)
    anywhere = pl.BlockSpec(memory_space=pl.ANY)
    local = jax.ShapeDtypeStruct((chans, width), BF16)
    signal = pltpu.VMEM((chans, width), BF16)
    one = pltpu.VMEM((rows, width), BF16)
    return pl.pallas_call(
        functools.partial(kernel, dp_count, ctx_count),
        out_shape=(local, local, local),
        in_specs=[anywhere] * 10,
        out_specs=(vmem, vmem, vmem),
        scratch_shapes=[signal] * 5
        + [signal, signal, signal, signal, one, signal, signal, one]
        + [pltpu.VMEM(t.shape, t.dtype) for t in constants]
        + [
            pltpu.SemaphoreType.DMA((5,)),
            pltpu.SemaphoreType.DMA((5,)),
            pltpu.SemaphoreType.DMA((6,)),
            pltpu.SemaphoreType.DMA((6,)),
        ],
        compiler_params=pltpu.CompilerParams(
            collective_id=0, has_side_effects=True, vmem_limit_bytes=60 * 1024 * 1024
        ),
        cost_estimate=pl.CostEstimate(
            flops=2_000_000_000, bytes_accessed=4_000_000, transcendentals=0
        ),
    )(outer, inner, values, cotan, filter_taps, *[jnp.asarray(t) for t in constants])


def on_device(gate_outer, gate_inner, values_in, cotangent, filter_taps, skip_gain):
    outer = gate_outer[0]
    inner = gate_inner[0]
    values = values_in[0]
    cotan = cotangent[0]
    ranks = lax.axis_size("ctx") * lax.axis_size("dp")
    mixed = (inner.astype(F32) * values.astype(F32)).astype(BF16)
    back_in = (cotan.astype(F32) * outer.astype(F32)).astype(BF16)
    if outer.shape[0] % (16 * ranks) == 0 and outer.shape[1] == inner_order:
        conv_seq, back_seq, filter_grad = kernel_exchange(outer, inner, values, cotan, filter_taps)
    else:
        conv_seq, back_seq, filter_grad = general_exchange(mixed, back_in, filter_taps)
    gain = skip_gain[:, None]
    state = conv_seq.astype(F32) + gain * mixed.astype(F32)
    layer = (outer.astype(F32) * state).astype(BF16)
    g_outer = (cotan.astype(F32) * state).astype(BF16)
    g_mixed = back_seq.astype(F32) + gain * back_in.astype(F32)
    g_inner = (g_mixed * values.astype(F32)).astype(BF16)
    g_values = (g_mixed * inner.astype(F32)).astype(BF16)
    return (layer[None], g_outer[None], g_inner[None], g_values[None], filter_grad.astype(F32))


def solution(mesh):
    placed = (
        P("dp", None, "ctx"),
        P("dp", None, "ctx"),
        P("dp", None, "ctx"),
        P("dp", None, "ctx"),
        P(None, "ctx"),
        P(),
    )
    return jax.shard_map(
        on_device,
        mesh=mesh,
        in_specs=placed,
        out_specs=(
            P("dp", None, "ctx"),
            P("dp", None, "ctx"),
            P("dp", None, "ctx"),
            P("dp", None, "ctx"),
            P(None, "ctx"),
        ),
        check_vma=False,
    )
```

```python
import functools
import math

import jax
import jax.numpy as jnp
import numpy as np
from jax import lax
from jax.experimental import pallas as pl
from jax.experimental.pallas import tpu as pltpu
from jax.sharding import PartitionSpec as P

highest = lax.Precision.HIGHEST
inner_order = 128
MESH = pl.DeviceIdType.MESH
F32 = jnp.float32
BF16 = jnp.bfloat16


def tables(order, count):
    rows = lax.broadcasted_iota(jnp.int32, (order, count), 0)
    cols = lax.broadcasted_iota(jnp.int32, (order, count), 1)
    angle = (rows * cols % order).astype(jnp.float32) * (2.0 * math.pi / order)
    return (jnp.cos(angle), jnp.sin(angle))


def twiddles(outer_order, total):
    rows = lax.broadcasted_iota(jnp.int32, (outer_order, inner_order), 0)
    cols = lax.broadcasted_iota(jnp.int32, (outer_order, inner_order), 1)
    angle = (rows * cols % total).astype(jnp.float32) * (2.0 * math.pi / total)
    return (jnp.cos(angle), jnp.sin(angle))


def forward_spectrum(signal):
    chans, seq = signal.shape
    outer_order = 2 * seq // inner_order
    half = outer_order // 2
    block_groups = signal.reshape(chans, half, inner_order)
    cos_p, sin_p = tables(outer_order, half)
    a_re = jnp.einsum("kn,cnm->ckm", cos_p, block_groups, precision=highest)
    a_im = -jnp.einsum("kn,cnm->ckm", sin_p, block_groups, precision=highest)
    tw_c, tw_s = twiddles(outer_order, outer_order * inner_order)
    b_re = a_re * tw_c + a_im * tw_s
    b_im = a_im * tw_c - a_re * tw_s
    cos_q, sin_q = tables(inner_order, inner_order)
    x_re = jnp.einsum("ckn,nm->ckm", b_re, cos_q, precision=highest) + jnp.einsum(
        "ckn,nm->ckm", b_im, sin_q, precision=highest
    )
    x_im = jnp.einsum("ckn,nm->ckm", b_im, cos_q, precision=highest) - jnp.einsum(
        "ckn,nm->ckm", b_re, sin_q, precision=highest
    )
    return (x_re, x_im)


def inverse_real_part(y_re, y_im):
    chans, outer_order, _ = y_re.shape
    half = outer_order // 2
    total = outer_order * inner_order
    cos_q, sin_q = tables(inner_order, inner_order)
    z_re = jnp.einsum("ckn,nm->ckm", y_re, cos_q, precision=highest) - jnp.einsum(
        "ckn,nm->ckm", y_im, sin_q, precision=highest
    )
    z_im = jnp.einsum("ckn,nm->ckm", y_im, cos_q, precision=highest) + jnp.einsum(
        "ckn,nm->ckm", y_re, sin_q, precision=highest
    )
    tw_c, tw_s = twiddles(outer_order, total)
    w_re = z_re * tw_c - z_im * tw_s
    w_im = z_im * tw_c + z_re * tw_s
    cos_p, sin_p = tables(outer_order, half)
    result = jnp.einsum("kn,ckm->cnm", cos_p, w_re, precision=highest) - jnp.einsum(
        "kn,ckm->cnm", sin_p, w_im, precision=highest
    )
    return (result * (1.0 / total)).reshape(chans, half * inner_order)


def general_exchange(mixed, back_in, filter_taps):
    ctx_count = lax.axis_size("ctx")
    dp_count = lax.axis_size("dp")
    seq = mixed.shape[1] * ctx_count
    norm_scale = 1.0 / math.sqrt(dp_count * seq)
    mixed_ch, back_ch, taps_ch = (
        lax.all_to_all(mixed, "ctx", split_axis=0, concat_axis=1, tiled=True),
        lax.all_to_all(back_in, "ctx", split_axis=0, concat_axis=1, tiled=True),
        lax.all_to_all(filter_taps, "ctx", split_axis=0, concat_axis=1, tiled=True),
    )
    h_re, h_im = forward_spectrum(taps_ch.astype(jnp.float32))
    u_re, u_im = forward_spectrum(mixed_ch.astype(jnp.float32))
    d_re, d_im = forward_spectrum(back_ch.astype(jnp.float32))
    conv_ch = inverse_real_part(u_re * h_re - u_im * h_im, u_re * h_im + u_im * h_re).astype(
        jnp.bfloat16
    )
    back_ch_out = inverse_real_part(h_re * d_re + h_im * d_im, h_re * d_im - h_im * d_re).astype(
        jnp.bfloat16
    )
    conv_seq, back_seq = (
        lax.all_to_all(conv_ch, "ctx", split_axis=1, concat_axis=0, tiled=True),
        lax.all_to_all(back_ch_out, "ctx", split_axis=1, concat_axis=0, tiled=True),
    )
    g_re = d_re * u_re + d_im * u_im
    g_im = d_im * u_re - d_re * u_im
    term = inverse_real_part(g_re, g_im)
    summed = lax.psum(term, "dp")
    filter_grad = lax.all_to_all(
        summed * norm_scale, "ctx", split_axis=1, concat_axis=0, tiled=True
    )
    return conv_seq, back_seq, filter_grad


def rounded(table):
    return np.asarray(table.astype(np.float32).astype(BF16))


@functools.lru_cache(maxsize=None)
def kernel_tables(blocks, group, width):
    total = 2 * blocks * width
    n = np.arange(blocks)
    angle = 2.0 * np.pi * ((np.outer(2 * n + 1, n)) % (4 * blocks)) / (4 * blocks)
    unit = np.eye(group)
    outer_f = np.concatenate([np.kron(np.cos(angle), unit), np.kron(-np.sin(angle), unit)], axis=0)
    outer_i = outer_f.T * (2.0 / total)
    m = np.arange(width)
    angle_in = 2.0 * np.pi * (np.outer(m, m) % width) / width
    c, s = np.cos(angle_in), np.sin(angle_in)
    inner_f = np.block([[c, -s], [s, c]])
    inner_i = np.block([[c, s], [-s, c]])
    angle_tw = 2.0 * np.pi * np.outer(2 * n + 1, m) / (2.0 * total)
    tw = np.stack([np.cos(angle_tw), np.sin(angle_tw)])
    tw = np.repeat(tw, group, axis=1).astype(np.float32)
    return rounded(outer_f), rounded(outer_i), rounded(inner_f), rounded(inner_i), tw


def dot(a, b):
    return jnp.dot(a, b, preferred_element_type=F32)


def kernel(
    dp_count,
    ctx_count,
    outer_hbm,
    inner_hbm,
    values_hbm,
    cotan_hbm,
    taps_hbm,
    outer_f_hbm,
    outer_i_hbm,
    inner_f_hbm,
    inner_i_hbm,
    tw_hbm,
    gain_hbm,
    state_out,
    g_mixed_out,
    grad_out,
    outer_ref,
    inner_ref,
    values_ref,
    cotan_ref,
    taps_ref,
    pair,
    recv_pair,
    recv_h,
    sent_pair,
    result_pair,
    sent_grad,
    gain_ref,
    outer_f,
    outer_i,
    inner_f,
    inner_i,
    tw,
    input_sems,
    table_sems,
    send_sems,
    recv_sems,
):
    ranks = dp_count * ctx_count
    chans, width = taps_ref.shape
    group = chans // ranks
    rows = ctx_count * group
    my_dp = lax.axis_index("dp")
    my_ctx = lax.axis_index("ctx")
    me = my_dp * ctx_count + my_ctx

    input_copies = [
        pltpu.make_async_copy(src, dst, input_sems.at[i])
        for i, (src, dst) in enumerate(
            [
                (inner_hbm, inner_ref),
                (values_hbm, values_ref),
                (taps_hbm, taps_ref),
                (cotan_hbm, cotan_ref),
                (outer_hbm, outer_ref),
            ]
        )
    ]
    for copy in input_copies:
        copy.start()
    barrier = pltpu.get_barrier_semaphore()

    def greet(i, carry):
        peer = lax.rem(me + i, ranks)
        pl.semaphore_signal(
            barrier,
            inc=1,
            device_id=(peer // ctx_count, lax.rem(peer, ctx_count)),
            device_id_type=MESH,
        )
        return carry

    lax.fori_loop(1, ranks, greet, 0)

    table_copies = [
        pltpu.make_async_copy(src, dst, table_sems.at[i])
        for i, (src, dst) in enumerate(
            [
                (outer_f_hbm, outer_f),
                (inner_f_hbm, inner_f),
                (tw_hbm, tw),
                (inner_i_hbm, inner_i),
                (outer_i_hbm, outer_i),
                (gain_hbm, gain_ref),
            ]
        )
    ]
    for copy in table_copies:
        copy.start()

    for copy in input_copies:
        copy.wait()
    def by_peer(x):
        return x.reshape(ranks, group, width)

    pair[:, :group] = by_peer(
        (inner_ref[...].astype(F32) * values_ref[...].astype(F32)).astype(BF16)
    )
    pair[:, group:] = by_peer(
        (cotan_ref[...].astype(F32) * outer_ref[...].astype(F32)).astype(BF16)
    )
    pl.semaphore_wait(barrier, ranks - 1)

    def chunk(ref, index):
        return ref.at[pl.ds(pl.multiple_of(index * group, group), group)]

    def to_peer(src, dst, which, peer):
        return pltpu.make_async_remote_copy(
            src_ref=src,
            dst_ref=dst,
            send_sem=send_sems.at[which],
            recv_sem=recv_sems.at[which],
            device_id=(peer // ctx_count, lax.rem(peer, ctx_count)),
            device_id_type=MESH,
        )

    def target(step):
        pair = step // dp_count
        half = (pair + 1) // 2
        sign = 1 - 2 * lax.rem(pair + 1, 2)
        ctx = lax.rem(my_ctx + ctx_count // 2 + sign * half + ctx_count, ctx_count)
        dp = lax.rem(my_dp + lax.rem(step, dp_count) + 1, dp_count)
        return dp, ctx

    def send_taps(i, carry):
        half = (i + 1) // 2
        sign = 1 - 2 * lax.rem(i + 1, 2)
        ctx = lax.rem(my_ctx + ctx_count // 2 + sign * half + ctx_count, ctx_count)
        peer = my_dp * ctx_count + ctx
        to_peer(chunk(taps_ref, peer), chunk(recv_h, my_ctx), 0, peer).start()
        return carry

    def send_pairs(src, dst, which):
        def step(i, carry):
            dp, ctx = target(i)
            peer = dp * ctx_count + ctx
            to_peer(src.at[peer], dst.at[me], which, peer).start()
            return carry

        lax.fori_loop(0, ranks - 1, step, 0)
        pltpu.make_async_copy(src.at[me], dst.at[me], recv_sems.at[which]).start()

    send_pairs(pair, recv_pair, 1)
    lax.fori_loop(0, ctx_count - 1, send_taps, 0)
    pltpu.make_async_copy(chunk(taps_ref, me), chunk(recv_h, my_ctx), recv_sems.at[0]).start()

    def arrived(ref, which):
        pltpu.make_async_copy(ref, ref, recv_sems.at[which]).wait()

    def spectra(signals):
        count = len(signals)
        side = jnp.concatenate(signals, axis=1)
        a = dot(outer_f[...], side)
        parts = []
        for s in range(count):
            re = a[:rows, s * width : (s + 1) * width]
            im = a[rows:, s * width : (s + 1) * width]
            parts.append(
                jnp.concatenate([re * tw[0] + im * tw[1], im * tw[0] - re * tw[1]], axis=1)
            )
        x = dot(jnp.concatenate(parts, axis=0).astype(BF16), inner_f[...])
        return [
            (x[s * rows : (s + 1) * rows, :width], x[s * rows : (s + 1) * rows, width:])
            for s in range(count)
        ]

    def signals_of(products):
        count = len(products)
        side = jnp.concatenate([jnp.concatenate([re, im], axis=1) for re, im in products], axis=0)
        z = dot(side.astype(BF16), inner_i[...])
        parts = []
        for s in range(count):
            re = z[s * rows : (s + 1) * rows, :width]
            im = z[s * rows : (s + 1) * rows, width:]
            parts.append(
                jnp.concatenate([re * tw[0] - im * tw[1], im * tw[0] + re * tw[1]], axis=0)
            )
        y = dot(outer_i[...], jnp.concatenate(parts, axis=1).astype(BF16))
        return [y[:, s * width : (s + 1) * width] for s in range(count)]

    def times(a, b):
        return a[0] * b[0] - a[1] * b[1], a[0] * b[1] + a[1] * b[0]

    def times_conj(a, b):
        return a[0] * b[0] + a[1] * b[1], a[1] * b[0] - a[0] * b[1]

    def sequence(s, part):
        block = recv_pair[s * ctx_count : (s + 1) * ctx_count, part * group : (part + 1) * group]
        return block.reshape(rows, width)

    def keep(s, part, y):
        sent_pair[s * ctx_count : (s + 1) * ctx_count, part * group : (part + 1) * group] = (
            y.astype(BF16).reshape(ctx_count, group, width)
        )

    arrived(recv_pair, 1)
    for copy in table_copies:
        copy.wait()
    spec_u = spectra([sequence(s, 0) for s in range(dp_count)])
    spec_d = spectra([sequence(s, 1) for s in range(dp_count)])
    terms = [times_conj(d, u) for d, u in zip(spec_d, spec_u)]
    term = (sum(t[0] for t in terms), sum(t[1] for t in terms))
    norm_scale = 1.0 / math.sqrt(dp_count * ctx_count * width)
    sent_grad[...] = (signals_of([term])[0] * norm_scale).astype(BF16)

    def send_grad(i, carry):
        half = (i + 1) // 2
        sign = 1 - 2 * lax.rem(i + 1, 2)
        ctx = lax.rem(my_ctx + ctx_count // 2 + sign * half + ctx_count, ctx_count)
        peer = my_dp * ctx_count + ctx
        to_peer(chunk(sent_grad, ctx), chunk(grad_out, me), 3, peer).start()
        return carry

    lax.fori_loop(0, ctx_count - 1, send_grad, 0)
    pltpu.make_async_copy(chunk(sent_grad, my_ctx), chunk(grad_out, me), recv_sems.at[3]).start()

    arrived(recv_h, 0)
    spec_h = spectra([recv_h[...]])[0]
    for s, y in enumerate(signals_of([times(u, spec_h) for u in spec_u])):
        keep(s, 0, y)
    for s, y in enumerate(signals_of([times_conj(d, spec_h) for d in spec_d])):
        keep(s, 1, y)
    send_pairs(sent_pair, result_pair, 2)
    def share(ref, dp):
        return ref.at[pl.ds(pl.multiple_of(dp * rows, rows), rows)]

    mine = share(grad_out, my_dp)
    arrived(mine, 3)
    forwards = [
        to_peer(mine, mine, 3 + i, lax.rem(my_dp + i, dp_count) * ctx_count + my_ctx)
        for i in range(1, dp_count)
    ]
    for copy in forwards:
        copy.start()

    per = width // group

    def gain_of(t):
        return jnp.broadcast_to(gain_ref[t * width : (t + 1) * width][None, :], (width, width)).T

    arrived(result_pair, 2)
    for t in range(chans // width):
        gain = gain_of(t)
        for part, out in ((0, state_out), (1, g_mixed_out)):
            which = (slice(t * per, (t + 1) * per), slice(part * group, (part + 1) * group))
            signal = pair[which].reshape(width, width).astype(F32)
            result = result_pair[which].reshape(width, width).astype(F32)
            out[t * width : (t + 1) * width] = result + gain * signal
    for copy in forwards:
        copy.wait()
    taps_sent = taps_ref.at[pl.ds(0, (ctx_count - 1) * group)]
    pairs_sent = pair.at[pl.ds(0, ranks - 1)]
    for which, part in ((0, taps_sent), (1, pairs_sent), (2, pairs_sent), (3, taps_sent)):
        pltpu.make_async_copy(part, part, send_sems.at[which]).wait()


def kernel_layer(outer, inner, values, cotan, filter_taps, gain):
    ctx_count = lax.axis_size("ctx")
    dp_count = lax.axis_size("dp")
    chans, width = outer.shape
    group = chans // (dp_count * ctx_count)
    rows = ctx_count * group
    constants = kernel_tables(ctx_count, group, width)
    vmem = pl.BlockSpec(memory_space=pltpu.VMEM)
    anywhere = pl.BlockSpec(memory_space=pl.ANY)
    local = jax.ShapeDtypeStruct((chans, width), BF16)
    signal = pltpu.VMEM((chans, width), BF16)
    one = pltpu.VMEM((rows, width), BF16)
    pair = pltpu.VMEM((dp_count * ctx_count, 2 * group, width), BF16)
    wide = jax.ShapeDtypeStruct((chans, width), F32)
    return pl.pallas_call(
        functools.partial(kernel, dp_count, ctx_count),
        out_shape=(wide, wide, local),
        in_specs=[anywhere] * 11,
        out_specs=(vmem, vmem, vmem),
        scratch_shapes=[signal] * 5
        + [pair, pair, one, pair, pair, one, pltpu.VMEM((chans,), F32)]
        + [pltpu.VMEM(t.shape, t.dtype) for t in constants]
        + [
            pltpu.SemaphoreType.DMA((5,)),
            pltpu.SemaphoreType.DMA((6,)),
            pltpu.SemaphoreType.DMA((3 + dp_count,)),
            pltpu.SemaphoreType.DMA((3 + dp_count,)),
        ],
        compiler_params=pltpu.CompilerParams(
            collective_id=0, has_side_effects=True, vmem_limit_bytes=60 * 1024 * 1024
        ),
        cost_estimate=pl.CostEstimate(
            flops=2_000_000_000, bytes_accessed=4_000_000, transcendentals=0
        ),
    )(outer, inner, values, cotan, filter_taps, *[jnp.asarray(t) for t in constants], gain)


def on_device(gate_outer, gate_inner, values_in, cotangent, filter_taps, skip_gain):
    outer = gate_outer[0]
    inner = gate_inner[0]
    values = values_in[0]
    cotan = cotangent[0]
    ranks = lax.axis_size("ctx") * lax.axis_size("dp")
    chans, width = outer.shape
    if chans % (16 * ranks) == 0 and chans % width == 0 and width == inner_order:
        state, g_mixed, filter_grad = kernel_layer(
            outer, inner, values, cotan, filter_taps, skip_gain
        )
    else:
        mixed = (inner.astype(F32) * values.astype(F32)).astype(BF16)
        back_in = (cotan.astype(F32) * outer.astype(F32)).astype(BF16)
        conv_seq, back_seq, filter_grad = general_exchange(mixed, back_in, filter_taps)
        gain = skip_gain[:, None]
        state = conv_seq.astype(F32) + gain * mixed.astype(F32)
        g_mixed = back_seq.astype(F32) + gain * back_in.astype(F32)
    layer = (outer.astype(F32) * state).astype(BF16)
    g_outer = (cotan.astype(F32) * state).astype(BF16)
    g_inner = (g_mixed * values.astype(F32)).astype(BF16)
    g_values = (g_mixed * inner.astype(F32)).astype(BF16)
    return (layer[None], g_outer[None], g_inner[None], g_values[None], filter_grad.astype(F32))


def solution(mesh):
    placed = (
        P("dp", None, "ctx"),
        P("dp", None, "ctx"),
        P("dp", None, "ctx"),
        P("dp", None, "ctx"),
        P(None, "ctx"),
        P(),
    )
    return jax.shard_map(
        on_device,
        mesh=mesh,
        in_specs=placed,
        out_specs=(
            P("dp", None, "ctx"),
            P("dp", None, "ctx"),
            P("dp", None, "ctx"),
            P("dp", None, "ctx"),
            P(None, "ctx"),
        ),
        check_vma=False,
    )
```

```python
import functools
import math

import jax
import jax.numpy as jnp
import numpy as np
from jax import lax
from jax.experimental import pallas as pl
from jax.experimental.pallas import tpu as pltpu
from jax.sharding import PartitionSpec as P

highest = lax.Precision.HIGHEST
inner_order = 128
MESH = pl.DeviceIdType.MESH
F32 = jnp.float32
BF16 = jnp.bfloat16


def tables(order, count):
    rows = lax.broadcasted_iota(jnp.int32, (order, count), 0)
    cols = lax.broadcasted_iota(jnp.int32, (order, count), 1)
    angle = (rows * cols % order).astype(jnp.float32) * (2.0 * math.pi / order)
    return (jnp.cos(angle), jnp.sin(angle))


def twiddles(outer_order, total):
    rows = lax.broadcasted_iota(jnp.int32, (outer_order, inner_order), 0)
    cols = lax.broadcasted_iota(jnp.int32, (outer_order, inner_order), 1)
    angle = (rows * cols % total).astype(jnp.float32) * (2.0 * math.pi / total)
    return (jnp.cos(angle), jnp.sin(angle))


def forward_spectrum(signal):
    chans, seq = signal.shape
    outer_order = 2 * seq // inner_order
    half = outer_order // 2
    block_groups = signal.reshape(chans, half, inner_order)
    cos_p, sin_p = tables(outer_order, half)
    a_re = jnp.einsum("kn,cnm->ckm", cos_p, block_groups, precision=highest)
    a_im = -jnp.einsum("kn,cnm->ckm", sin_p, block_groups, precision=highest)
    tw_c, tw_s = twiddles(outer_order, outer_order * inner_order)
    b_re = a_re * tw_c + a_im * tw_s
    b_im = a_im * tw_c - a_re * tw_s
    cos_q, sin_q = tables(inner_order, inner_order)
    x_re = jnp.einsum("ckn,nm->ckm", b_re, cos_q, precision=highest) + jnp.einsum(
        "ckn,nm->ckm", b_im, sin_q, precision=highest
    )
    x_im = jnp.einsum("ckn,nm->ckm", b_im, cos_q, precision=highest) - jnp.einsum(
        "ckn,nm->ckm", b_re, sin_q, precision=highest
    )
    return (x_re, x_im)


def inverse_real_part(y_re, y_im):
    chans, outer_order, _ = y_re.shape
    half = outer_order // 2
    total = outer_order * inner_order
    cos_q, sin_q = tables(inner_order, inner_order)
    z_re = jnp.einsum("ckn,nm->ckm", y_re, cos_q, precision=highest) - jnp.einsum(
        "ckn,nm->ckm", y_im, sin_q, precision=highest
    )
    z_im = jnp.einsum("ckn,nm->ckm", y_im, cos_q, precision=highest) + jnp.einsum(
        "ckn,nm->ckm", y_re, sin_q, precision=highest
    )
    tw_c, tw_s = twiddles(outer_order, total)
    w_re = z_re * tw_c - z_im * tw_s
    w_im = z_im * tw_c + z_re * tw_s
    cos_p, sin_p = tables(outer_order, half)
    result = jnp.einsum("kn,ckm->cnm", cos_p, w_re, precision=highest) - jnp.einsum(
        "kn,ckm->cnm", sin_p, w_im, precision=highest
    )
    return (result * (1.0 / total)).reshape(chans, half * inner_order)


def general_exchange(mixed, back_in, filter_taps):
    ctx_count = lax.axis_size("ctx")
    dp_count = lax.axis_size("dp")
    seq = mixed.shape[1] * ctx_count
    norm_scale = 1.0 / math.sqrt(dp_count * seq)
    mixed_ch, back_ch, taps_ch = (
        lax.all_to_all(mixed, "ctx", split_axis=0, concat_axis=1, tiled=True),
        lax.all_to_all(back_in, "ctx", split_axis=0, concat_axis=1, tiled=True),
        lax.all_to_all(filter_taps, "ctx", split_axis=0, concat_axis=1, tiled=True),
    )
    h_re, h_im = forward_spectrum(taps_ch.astype(jnp.float32))
    u_re, u_im = forward_spectrum(mixed_ch.astype(jnp.float32))
    d_re, d_im = forward_spectrum(back_ch.astype(jnp.float32))
    conv_ch = inverse_real_part(u_re * h_re - u_im * h_im, u_re * h_im + u_im * h_re).astype(
        jnp.bfloat16
    )
    back_ch_out = inverse_real_part(h_re * d_re + h_im * d_im, h_re * d_im - h_im * d_re).astype(
        jnp.bfloat16
    )
    conv_seq, back_seq = (
        lax.all_to_all(conv_ch, "ctx", split_axis=1, concat_axis=0, tiled=True),
        lax.all_to_all(back_ch_out, "ctx", split_axis=1, concat_axis=0, tiled=True),
    )
    g_re = d_re * u_re + d_im * u_im
    g_im = d_im * u_re - d_re * u_im
    term = inverse_real_part(g_re, g_im)
    summed = lax.psum(term, "dp")
    filter_grad = lax.all_to_all(
        summed * norm_scale, "ctx", split_axis=1, concat_axis=0, tiled=True
    )
    return conv_seq, back_seq, filter_grad


def rounded(table):
    return np.asarray(table.astype(np.float32).astype(BF16))


@functools.lru_cache(maxsize=None)
def kernel_tables(blocks, group, width):
    total = 2 * blocks * width
    n = np.arange(blocks)
    angle = 2.0 * np.pi * ((np.outer(2 * n + 1, n)) % (4 * blocks)) / (4 * blocks)
    unit = np.eye(group)
    outer_f = np.concatenate([np.kron(np.cos(angle), unit), np.kron(-np.sin(angle), unit)], axis=0)
    outer_i = outer_f.T * (2.0 / total)
    m = np.arange(width)
    angle_in = 2.0 * np.pi * (np.outer(m, m) % width) / width
    c, s = np.cos(angle_in), np.sin(angle_in)
    inner_f = np.block([[c, -s], [s, c]])
    inner_i = np.block([[c, s], [-s, c]])
    angle_tw = 2.0 * np.pi * np.outer(2 * n + 1, m) / (2.0 * total)
    tw = np.stack([np.cos(angle_tw), np.sin(angle_tw)])
    tw = np.repeat(tw, group, axis=1).astype(np.float32)
    return rounded(outer_f), rounded(outer_i), rounded(inner_f), rounded(inner_i), tw


def dot(a, b):
    return jnp.dot(a, b, preferred_element_type=F32)


def kernel(
    dp_count,
    ctx_count,
    outer_hbm,
    inner_hbm,
    values_hbm,
    cotan_hbm,
    taps_hbm,
    outer_f_hbm,
    outer_i_hbm,
    inner_f_hbm,
    inner_i_hbm,
    tw_hbm,
    gain_hbm,
    state_out,
    g_mixed_out,
    grad_out,
    outer_ref,
    inner_ref,
    values_ref,
    cotan_ref,
    taps_ref,
    pair,
    recv_pair,
    recv_h,
    sent_pair,
    result_pair,
    sent_grad,
    gain_ref,
    outer_f,
    outer_i,
    inner_f,
    inner_i,
    tw,
    input_sems,
    table_sems,
    send_sems,
    recv_sems,
):
    ranks = dp_count * ctx_count
    chans, width = taps_ref.shape
    group = chans // ranks
    rows = ctx_count * group
    my_dp = lax.axis_index("dp")
    my_ctx = lax.axis_index("ctx")
    me = my_dp * ctx_count + my_ctx

    input_copies = [
        pltpu.make_async_copy(src, dst, input_sems.at[i])
        for i, (src, dst) in enumerate(
            [
                (inner_hbm, inner_ref),
                (values_hbm, values_ref),
                (taps_hbm, taps_ref),
                (cotan_hbm, cotan_ref),
                (outer_hbm, outer_ref),
            ]
        )
    ]
    for copy in input_copies:
        copy.start()
    barrier = pltpu.get_barrier_semaphore()

    def greet(i, carry):
        peer = lax.rem(me + i, ranks)
        pl.semaphore_signal(
            barrier,
            inc=1,
            device_id=(peer // ctx_count, lax.rem(peer, ctx_count)),
            device_id_type=MESH,
        )
        return carry

    lax.fori_loop(1, ranks, greet, 0)

    table_copies = [
        pltpu.make_async_copy(src, dst, table_sems.at[i])
        for i, (src, dst) in enumerate(
            [
                (outer_f_hbm, outer_f),
                (inner_f_hbm, inner_f),
                (tw_hbm, tw),
                (inner_i_hbm, inner_i),
                (outer_i_hbm, outer_i),
                (gain_hbm, gain_ref),
            ]
        )
    ]
    for copy in table_copies:
        copy.start()

    for copy in input_copies:
        copy.wait()
    def by_peer(x):
        return x.reshape(ranks, group, width)

    pair[:, :group] = by_peer(
        (inner_ref[...].astype(F32) * values_ref[...].astype(F32)).astype(BF16)
    )
    pair[:, group:] = by_peer(
        (cotan_ref[...].astype(F32) * outer_ref[...].astype(F32)).astype(BF16)
    )
    pl.semaphore_wait(barrier, ranks - 1)

    def chunk(ref, index):
        return ref.at[pl.ds(pl.multiple_of(index * group, group), group)]

    def to_peer(src, dst, which, peer):
        return pltpu.make_async_remote_copy(
            src_ref=src,
            dst_ref=dst,
            send_sem=send_sems.at[which],
            recv_sem=recv_sems.at[which],
            device_id=(peer // ctx_count, lax.rem(peer, ctx_count)),
            device_id_type=MESH,
        )

    def target(step):
        pair = step // dp_count
        half = (pair + 1) // 2
        sign = 1 - 2 * lax.rem(pair + 1, 2)
        ctx = lax.rem(my_ctx + ctx_count // 2 + sign * half + ctx_count, ctx_count)
        dp = lax.rem(my_dp + lax.rem(step, dp_count) + 1, dp_count)
        return dp, ctx

    def send_taps(i, carry):
        half = (i + 1) // 2
        sign = 1 - 2 * lax.rem(i + 1, 2)
        ctx = lax.rem(my_ctx + ctx_count // 2 + sign * half + ctx_count, ctx_count)
        peer = my_dp * ctx_count + ctx
        to_peer(chunk(taps_ref, peer), chunk(recv_h, my_ctx), 0, peer).start()
        return carry

    def send_pairs(src, dst, which):
        def step(i, carry):
            dp, ctx = target(i)
            peer = dp * ctx_count + ctx
            to_peer(src.at[peer], dst.at[me], which, peer).start()
            return carry

        lax.fori_loop(0, ranks - 1, step, 0)
        pltpu.make_async_copy(src.at[me], dst.at[me], recv_sems.at[which]).start()

    send_pairs(pair, recv_pair, 1)
    lax.fori_loop(0, ctx_count - 1, send_taps, 0)
    pltpu.make_async_copy(chunk(taps_ref, me), chunk(recv_h, my_ctx), recv_sems.at[0]).start()

    def arrived(ref, which):
        pltpu.make_async_copy(ref, ref, recv_sems.at[which]).wait()

    def spectra(signals):
        count = len(signals)
        side = jnp.concatenate(signals, axis=1)
        a = dot(outer_f[...], side)
        parts = []
        for s in range(count):
            re = a[:rows, s * width : (s + 1) * width]
            im = a[rows:, s * width : (s + 1) * width]
            parts.append(
                jnp.concatenate([re * tw[0] + im * tw[1], im * tw[0] - re * tw[1]], axis=1)
            )
        x = dot(jnp.concatenate(parts, axis=0).astype(BF16), inner_f[...])
        return [
            (x[s * rows : (s + 1) * rows, :width], x[s * rows : (s + 1) * rows, width:])
            for s in range(count)
        ]

    def signals_of(products):
        count = len(products)
        side = jnp.concatenate([jnp.concatenate([re, im], axis=1) for re, im in products], axis=0)
        z = dot(side.astype(BF16), inner_i[...])
        parts = []
        for s in range(count):
            re = z[s * rows : (s + 1) * rows, :width]
            im = z[s * rows : (s + 1) * rows, width:]
            parts.append(
                jnp.concatenate([re * tw[0] - im * tw[1], im * tw[0] + re * tw[1]], axis=0)
            )
        y = dot(outer_i[...], jnp.concatenate(parts, axis=1).astype(BF16))
        return [y[:, s * width : (s + 1) * width] for s in range(count)]

    def times(a, b):
        return a[0] * b[0] - a[1] * b[1], a[0] * b[1] + a[1] * b[0]

    def times_conj(a, b):
        return a[0] * b[0] + a[1] * b[1], a[1] * b[0] - a[0] * b[1]

    def sequence(s, part):
        block = recv_pair[s * ctx_count : (s + 1) * ctx_count, part * group : (part + 1) * group]
        return block.reshape(rows, width)

    def keep(s, part, y):
        sent_pair[s * ctx_count : (s + 1) * ctx_count, part * group : (part + 1) * group] = (
            y.astype(BF16).reshape(ctx_count, group, width)
        )

    arrived(recv_pair, 1)
    for copy in table_copies:
        copy.wait()
    spec = spectra([sequence(s, part) for part in range(2) for s in range(dp_count)])
    spec_u, spec_d = spec[:dp_count], spec[dp_count:]
    terms = [times_conj(d, u) for d, u in zip(spec_d, spec_u)]
    term = (sum(t[0] for t in terms), sum(t[1] for t in terms))
    norm_scale = 1.0 / math.sqrt(dp_count * ctx_count * width)
    sent_grad[...] = (signals_of([term])[0] * norm_scale).astype(BF16)

    def send_grad(i, carry):
        half = (i + 1) // 2
        sign = 1 - 2 * lax.rem(i + 1, 2)
        ctx = lax.rem(my_ctx + ctx_count // 2 + sign * half + ctx_count, ctx_count)
        peer = my_dp * ctx_count + ctx
        to_peer(chunk(sent_grad, ctx), chunk(grad_out, me), 3, peer).start()
        return carry

    lax.fori_loop(0, ctx_count - 1, send_grad, 0)
    pltpu.make_async_copy(chunk(sent_grad, my_ctx), chunk(grad_out, me), recv_sems.at[3]).start()

    arrived(recv_h, 0)
    spec_h = spectra([recv_h[...]])[0]
    results = signals_of(
        [times(u, spec_h) for u in spec_u] + [times_conj(d, spec_h) for d in spec_d]
    )
    for i, y in enumerate(results):
        keep(i % dp_count, i // dp_count, y)
    send_pairs(sent_pair, result_pair, 2)
    def share(ref, dp):
        return ref.at[pl.ds(pl.multiple_of(dp * rows, rows), rows)]

    mine = share(grad_out, my_dp)
    arrived(mine, 3)
    forwards = [
        to_peer(mine, mine, 3 + i, lax.rem(my_dp + i, dp_count) * ctx_count + my_ctx)
        for i in range(1, dp_count)
    ]
    for copy in forwards:
        copy.start()

    per = width // group

    def gain_of(t):
        return jnp.broadcast_to(gain_ref[t * width : (t + 1) * width][None, :], (width, width)).T

    arrived(result_pair, 2)
    for t in range(chans // width):
        gain = gain_of(t)
        for part, out in ((0, state_out), (1, g_mixed_out)):
            which = (slice(t * per, (t + 1) * per), slice(part * group, (part + 1) * group))
            signal = pair[which].reshape(width, width).astype(F32)
            result = result_pair[which].reshape(width, width).astype(F32)
            out[t * width : (t + 1) * width] = result + gain * signal
    for copy in forwards:
        copy.wait()
    taps_sent = taps_ref.at[pl.ds(0, (ctx_count - 1) * group)]
    pairs_sent = pair.at[pl.ds(0, ranks - 1)]
    for which, part in ((0, taps_sent), (1, pairs_sent), (2, pairs_sent), (3, taps_sent)):
        pltpu.make_async_copy(part, part, send_sems.at[which]).wait()


def kernel_layer(outer, inner, values, cotan, filter_taps, gain):
    ctx_count = lax.axis_size("ctx")
    dp_count = lax.axis_size("dp")
    chans, width = outer.shape
    group = chans // (dp_count * ctx_count)
    rows = ctx_count * group
    constants = kernel_tables(ctx_count, group, width)
    vmem = pl.BlockSpec(memory_space=pltpu.VMEM)
    anywhere = pl.BlockSpec(memory_space=pl.ANY)
    local = jax.ShapeDtypeStruct((chans, width), BF16)
    signal = pltpu.VMEM((chans, width), BF16)
    one = pltpu.VMEM((rows, width), BF16)
    pair = pltpu.VMEM((dp_count * ctx_count, 2 * group, width), BF16)
    wide = jax.ShapeDtypeStruct((chans, width), F32)
    return pl.pallas_call(
        functools.partial(kernel, dp_count, ctx_count),
        out_shape=(wide, wide, local),
        in_specs=[anywhere] * 11,
        out_specs=(vmem, vmem, vmem),
        scratch_shapes=[signal] * 5
        + [pair, pair, one, pair, pair, one, pltpu.VMEM((chans,), F32)]
        + [pltpu.VMEM(t.shape, t.dtype) for t in constants]
        + [
            pltpu.SemaphoreType.DMA((5,)),
            pltpu.SemaphoreType.DMA((6,)),
            pltpu.SemaphoreType.DMA((3 + dp_count,)),
            pltpu.SemaphoreType.DMA((3 + dp_count,)),
        ],
        compiler_params=pltpu.CompilerParams(
            collective_id=0, has_side_effects=True, vmem_limit_bytes=60 * 1024 * 1024
        ),
        cost_estimate=pl.CostEstimate(
            flops=2_000_000_000, bytes_accessed=4_000_000, transcendentals=0
        ),
    )(outer, inner, values, cotan, filter_taps, *[jnp.asarray(t) for t in constants], gain)


def on_device(gate_outer, gate_inner, values_in, cotangent, filter_taps, skip_gain):
    outer = gate_outer[0]
    inner = gate_inner[0]
    values = values_in[0]
    cotan = cotangent[0]
    ranks = lax.axis_size("ctx") * lax.axis_size("dp")
    chans, width = outer.shape
    if chans % (16 * ranks) == 0 and chans % width == 0 and width == inner_order:
        state, g_mixed, filter_grad = kernel_layer(
            outer, inner, values, cotan, filter_taps, skip_gain
        )
    else:
        mixed = (inner.astype(F32) * values.astype(F32)).astype(BF16)
        back_in = (cotan.astype(F32) * outer.astype(F32)).astype(BF16)
        conv_seq, back_seq, filter_grad = general_exchange(mixed, back_in, filter_taps)
        gain = skip_gain[:, None]
        state = conv_seq.astype(F32) + gain * mixed.astype(F32)
        g_mixed = back_seq.astype(F32) + gain * back_in.astype(F32)
    layer = (outer.astype(F32) * state).astype(BF16)
    g_outer = (cotan.astype(F32) * state).astype(BF16)
    g_inner = (g_mixed * values.astype(F32)).astype(BF16)
    g_values = (g_mixed * inner.astype(F32)).astype(BF16)
    return (layer[None], g_outer[None], g_inner[None], g_values[None], filter_grad.astype(F32))


def solution(mesh):
    placed = (
        P("dp", None, "ctx"),
        P("dp", None, "ctx"),
        P("dp", None, "ctx"),
        P("dp", None, "ctx"),
        P(None, "ctx"),
        P(),
    )
    return jax.shard_map(
        on_device,
        mesh=mesh,
        in_specs=placed,
        out_specs=(
            P("dp", None, "ctx"),
            P("dp", None, "ctx"),
            P("dp", None, "ctx"),
            P("dp", None, "ctx"),
            P(None, "ctx"),
        ),
        check_vma=False,
    )
```
